32 devices in a mesh: parts: 2 (over x), lon: 16 (over z, y, core).
Axes of the slice: x: 2, y: 2, z: 4, core: 2. Of those that a mesh axis runs over, the one named last changes fastest.
Arguments:
- solution: float32 [2048, 32, 512], P(('parts', 'lon')), parts along dimension 0, may hold values from -6 to 6
- residual: float32 [2048, 32, 512], P(('parts', 'lon')), parts along dimension 0, may hold values from -12 to 12
- direction: float32 [2048, 32, 512], P(('parts', 'lon')), parts along dimension 0, may hold values from -12 to 12
- land: int32 [2048, 512], P(('parts', 'lon')), parts along dimension 0, may hold values 0 or 1
- clear: int32 [2048, 32, 512], P(('parts', 'lon')), parts along dimension 0, may hold values 0 or 1
- days: int32 [64], P('parts'), parts along dimension 0, may hold values from 0 to 63, as said below
- mixture: float32 [6, 3, 4], P('parts'), parts along dimension 0, may hold values from 0 to 1024, as said below
- q_lon: bfloat16 [1024, 1024], replicated, may hold values from -0.1875 to 0.1875
- q_lat: bfloat16 [512, 512], replicated, may hold values from -0.25 to 0.25
- q_day: bfloat16 [64, 32], P('parts'), parts along dimension 0, may hold values from -1 to 1
- lam_lon: float32 [1024], replicated, may hold values from 0.2 to 5
- lam_lat: float32 [512], replicated, may hold values from 0.2 to 5
- lam_day: float32 [64], P('parts'), parts along dimension 0, may hold values from 0.2 to 5
- noise: float32 [2], P('parts'), parts along dimension 0, may hold values from 0.5 to 2
- rz_mean: float32 [2], P('parts'), parts along dimension 0, may hold values from 0.25 to 1
Outputs:
- new_solution: float32 [2048, 32, 512], P(('parts', 'lon')), parts along dimension 0
- new_residual: float32 [2048, 32, 512], P(('parts', 'lon')), parts along dimension 0
- new_direction: float32 [2048, 32, 512], P(('parts', 'lon')), parts along dimension 0
- new_rz_mean: float32 [2], P('parts'), parts along dimension 0
The draws below stay inside these ranges and needn't reach their ends.
There are 2 independent parts, one for each index of `parts`. The reference program is written for one: setup_inputs(seed, part) draws one part's arguments, and reference() takes and returns one part's arrays. A program takes and returns all parts, laid end to end along the dimension named above; an argument that names none is the same for every part. Nothing has to cross between parts.
Inputs may be any that keep to these rules, and one draw needn't show every extreme that they name: days[k] is 2 k or 2 k + 1, so the days rise strictly within a record of 64 days; the first is 0 and the last 63. mixture[g, 0] are positive weights, mixture[g, 1] frequencies of at most one half per cell or day, mixture[g, 2] positive length scales in cells or days.
All inputs are finite; a program needn't handle non-finite values. No bound on the sum of `land` or of `clear` on one device may be relied on, other than what follows from the above.
Results may differ from the reference program's by a relative error of at most 0.0018.
Values may be sent and summed in bfloat16 or wider, within the bound.
A program may use at most 128 MiB of HBM per device.

```python
import math
import jax
import jax.numpy as jnp
from jax import lax

NLON = 1024
NLAT = 512
NT = 32
NQ = 4


def rough_field(key):
    keys = jax.random.split(key, 1)
    lon_pos = jnp.arange(NLON, dtype=jnp.float32)[:, None, None] / (NLON - 1)
    amplitude = jnp.exp(jnp.log(3.0) * lon_pos)
    values = jax.random.normal(keys[0], (NLON, NT, NLAT), jnp.float32) * amplitude
    return jnp.clip(values, -12.0, 12.0)


def draw_residual(key, part):
    return rough_field(jax.random.fold_in(key, 11))


def draw_direction(key, part):
    return rough_field(jax.random.fold_in(key, 23))


def draw_days(key, part):
    position = jnp.arange(NT)
    coin = jax.random.randint(key, (NT,), 0, 2)
    coin = jnp.where(position == 0, 0, jnp.where(position == NT - 1, 1, coin))
    return (2 * position + coin).astype(jnp.int32)


def draw_mixture(key, part):
    keys = jax.random.split(key, 3)
    spans = jnp.array([NLON, NLAT, 2 * NT], jnp.float32)[:, None]
    order = jnp.arange(NQ)[None, :]
    first = order == 0
    second = order == 1
    pick = jax.random.uniform(keys[0], (3, NQ), jnp.float32)
    short_top = jnp.log(spans / 8.0)
    short = jnp.exp(jnp.log(0.7) + pick * (short_top - jnp.log(0.7)))
    middle_low = jnp.log(jnp.maximum(spans / 64.0, 0.7))
    middle = jnp.exp(middle_low + pick * jnp.log(8.0))
    far = jnp.exp(jnp.log(spans / 4.0) + pick * jnp.log(4.0))
    scales = jnp.where(first, far, jnp.where(second, middle, short))
    raw = jax.random.uniform(keys[1], (3, NQ), jnp.float32)
    weights = jnp.exp(jnp.log(0.3) + raw * (jnp.log(0.8) - jnp.log(0.3))) / jnp.sqrt(scales)
    turn = jax.random.uniform(keys[2], (3, NQ), jnp.float32)
    freqs = turn * 0.5 / jnp.where(first, scales, 1.0)
    return jnp.stack([weights, freqs, scales], axis=1)


def with_ends(drawn, rng, least, high):
    place = [jax.random.randint(jax.random.fold_in(rng, axis), (), 0, length) for axis, length in enumerate(drawn.shape)]
    longest = drawn.shape.index(max(drawn.shape))
    beside = place[:longest] + [(place[longest] + 1) % drawn.shape[longest]] + place[longest + 1:]
    return drawn.at[tuple(place)].set(least).at[tuple(beside)].set(high)


def levels(own_key, dims, shards, low, high):
    def one(dim, shards_of):
        heights = jax.random.uniform(jax.random.fold_in(jax.random.fold_in(own_key, 6), dim), (shards_of,), jnp.float32, low / len(shards), high / len(shards))
        return jnp.repeat(jnp.exp(heights), dims[dim] // shards_of).reshape((-1,) + (1,) * (len(dims) - dim - 1))

    level = one(*shards[0])
    for cut in shards[1:]:
        level = level * one(*cut)
    return level


def normal_values(own_key, shape, deviation, reach, shards=(), kind=jnp.bfloat16):
    values = deviation * jax.random.normal(own_key, shape, jnp.float32)
    if shards:
        values = values * levels(own_key, shape, shards, -0.22, 0.18)
    return jnp.clip(values, -reach, reach).astype(kind)


def setup_inputs(seed: int = 0, part: int = 0) -> dict:
    splits = jax.random.split(jax.random.key(seed), 16)
    part_keys = jax.random.split(jax.random.fold_in(splits[15], part), 16)
    solution = normal_values(part_keys[0], (NLON, NT, NLAT), 1.0, 6.0, ((0, 16),), jnp.float32)
    residual = draw_residual(jax.random.fold_in(jax.random.fold_in(splits[15], part), 71), part)
    direction = draw_direction(jax.random.fold_in(jax.random.fold_in(splits[15], part), 71), part)
    land = with_ends((jax.random.randint(part_keys[3], (NLON, NLAT), 0, 3) < 2).astype(jnp.int32), jax.random.fold_in(part_keys[3], 1), 0, 1)
    clear = with_ends((jax.random.randint(part_keys[4], (NLON, NT, NLAT), 0, 4) < 3).astype(jnp.int32), jax.random.fold_in(part_keys[4], 1), 0, 1)
    days = draw_days(jax.random.fold_in(jax.random.fold_in(splits[15], part), 71), part)
    mixture = draw_mixture(jax.random.fold_in(jax.random.fold_in(splits[15], part), 71), part)
    q_lon = normal_values(splits[7], (NLON, NLON), NLON ** -0.5, 0.1875)
    q_lat = normal_values(splits[8], (NLAT, NLAT), NLAT ** -0.5, 0.25)
    q_day = normal_values(part_keys[9], (NT, NT), NT ** -0.5, 1.0)
    lam_lon = jnp.clip(jnp.exp(jax.random.uniform(splits[10], (NLON,), jnp.float32, math.log(0.2), math.log(5.0))), 0.2, 5.0)
    lam_lat = jnp.clip(jnp.exp(jax.random.uniform(splits[11], (NLAT,), jnp.float32, math.log(0.2), math.log(5.0))), 0.2, 5.0)
    lam_day = jnp.clip(jnp.exp(jax.random.uniform(part_keys[12], (NT,), jnp.float32, math.log(0.2), math.log(5.0))), 0.2, 5.0)
    noise = jnp.clip(jnp.exp(jax.random.uniform(part_keys[13], (1,), jnp.float32, math.log(0.5), math.log(2.0))), 0.5, 2.0)
    rz_mean = jnp.clip(jnp.exp(jax.random.uniform(part_keys[14], (1,), jnp.float32, math.log(0.25), math.log(1.0))), 0.25, 1.0)
    return dict(solution=solution, residual=residual, direction=direction, land=land, clear=clear, days=days, mixture=mixture, q_lon=q_lon, q_lat=q_lat, q_day=q_day, lam_lon=lam_lon, lam_lat=lam_lat, lam_day=lam_day, noise=noise, rz_mean=rz_mean)


def kernel_factor(left, right, params):
    diff = left[:, None] - right[None, :]
    total = jnp.zeros(diff.shape, jnp.float32)
    for comp in range(params.shape[1]):
        weight = params[0, comp]
        freq = params[1, comp]
        length = params[2, comp]
        ratio = diff / length
        total = total + weight * jnp.exp(-0.5 * ratio * ratio) * jnp.cos(2.0 * math.pi * freq * diff)
    return total.astype(jnp.bfloat16)


def day_apply(matrix, field):
    return jnp.einsum("ck,akb->acb", matrix.astype(jnp.float32), field.astype(jnp.float32), precision=lax.Precision.HIGHEST)


def lat_apply(matrix, field):
    return jnp.einsum("acj,bj->acb", field.astype(jnp.float32), matrix.astype(jnp.float32), precision=lax.Precision.HIGHEST)


def lon_apply(matrix, field):
    flat = field.reshape(field.shape[0], -1)
    return jnp.dot(matrix, flat, preferred_element_type=jnp.float32).reshape(field.shape)


def reference(solution, residual, direction, land, clear, days, mixture, q_lon, q_lat, q_day, lam_lon, lam_lat, lam_day, noise, rz_mean):
    bf = jnp.bfloat16
    cells = NLON * NT * NLAT
    observed = (land[:, None, :] * clear).astype(jnp.float32)
    sigma = noise[0]
    lon_pos = jnp.arange(NLON, dtype=jnp.float32)
    lat_pos = jnp.arange(NLAT, dtype=jnp.float32)
    day_pos = days.astype(jnp.float32)
    k_lon = kernel_factor(lon_pos, lon_pos, mixture[0])
    k_lat = kernel_factor(lat_pos, lat_pos, mixture[1])
    k_day = kernel_factor(day_pos, day_pos, mixture[2])

    first = (observed * direction).astype(bf)
    second = day_apply(k_day, first).astype(bf)
    third = lat_apply(k_lat, second).astype(bf)
    fourth = lon_apply(k_lon, third).astype(bf)
    image = observed * (fourth.astype(jnp.float32) + sigma * direction)
    curvature = jnp.sum(direction * image)
    alpha = rz_mean[0] * cells / curvature
    new_solution = solution + alpha * direction
    new_residual = residual - alpha * image

    g_zero = (observed * new_residual).astype(bf)
    g_one = day_apply(q_day.T, g_zero).astype(bf)
    g_two = lat_apply(q_lat.T, g_one).astype(bf)
    g_three = lon_apply(q_lon.T, g_two).astype(bf)
    denom = lam_lon[:, None, None] * lam_day[None, :, None] * lam_lat[None, None, :] + sigma
    scaled = (g_three.astype(jnp.float32) / denom).astype(bf)
    h_one = lon_apply(q_lon, scaled).astype(bf)
    h_two = lat_apply(q_lat, h_one).astype(bf)
    precond = observed * day_apply(q_day, h_two)
    new_rz = jnp.sum(new_residual * precond) / cells
    new_direction = precond + (new_rz / rz_mean[0]) * direction
    return (new_solution, new_residual, new_direction, new_rz.reshape(1))
```

```python
import functools
import math

import jax
import jax.numpy as jnp
from jax import lax
from jax.experimental import pallas as pl
from jax.experimental.pallas import tpu as pltpu
from jax.sharding import PartitionSpec as P

GROUP = 16
BLOCK = 128
BF = jnp.bfloat16
F32 = jnp.float32


def kernel_values(diff, params):
    total = jnp.zeros(diff.shape, F32)
    for comp in range(params.shape[1]):
        weight = params[0, comp]
        freq = params[1, comp]
        length = params[2, comp]
        ratio = diff / length
        total = total + weight * jnp.exp(-0.5 * ratio * ratio) * jnp.cos(
            2.0 * math.pi * freq * diff
        )
    return total


def toeplitz_kernel(w_ref, out_ref):
    n = out_ref.shape[0]
    wide = jnp.broadcast_to(w_ref[...], (BLOCK, 2 * n))
    rolled = pltpu.roll(wide, 0, 1, stride=1, stride_axis=0)
    for blk in range(n // BLOCK):
        lo = n - BLOCK * blk
        out_ref[BLOCK * blk : BLOCK * (blk + 1), :] = rolled[:, lo : lo + n].astype(BF)


def toeplitz_factor(n, params):
    diff = (jnp.arange(2 * n, dtype=F32) - n)[None, :]
    row = kernel_values(diff, params)
    return pl.pallas_call(
        toeplitz_kernel,
        out_shape=jax.ShapeDtypeStruct((n, n), BF),
        compiler_params=pltpu.CompilerParams(vmem_limit_bytes=24 * 1024 * 1024),
    )(row)


def allsum_kernel(n, x_ref, out_ref, buf, send_sem, recv_sem):
    me = lax.axis_index("lon")
    barrier = pltpu.get_barrier_semaphore()

    def greet(p, carry):
        peer = lax.rem(me + p, n)
        pl.semaphore_signal(
            barrier, inc=1, device_id={"lon": peer}, device_id_type=pl.DeviceIdType.MESH
        )
        return carry

    lax.fori_loop(1, n, greet, 0)
    pl.semaphore_wait(barrier, n - 1)

    def copy_to(p):
        return pltpu.make_async_remote_copy(
            src_ref=x_ref,
            dst_ref=buf.at[me],
            send_sem=send_sem.at[p],
            recv_sem=recv_sem.at[p],
            device_id={"lon": lax.rem(me + p, n)},
            device_id_type=pl.DeviceIdType.MESH,
        )

    def start(p, carry):
        copy_to(p).start()
        return carry

    lax.fori_loop(1, n, start, 0)
    buf[pl.ds(me, 1)] = x_ref[...][None]

    def finish(p, carry):
        copy_to(p).wait()
        return carry

    lax.fori_loop(1, n, finish, 0)
    out_ref[...] = jnp.sum(buf[...], axis=0)


def all_sum(value, n, ident):
    tile = jnp.full((8, 128), value, F32)
    out = pl.pallas_call(
        functools.partial(allsum_kernel, n),
        out_shape=jax.ShapeDtypeStruct((8, 128), F32),
        in_specs=[pl.BlockSpec(memory_space=pltpu.VMEM)],
        out_specs=pl.BlockSpec(memory_space=pltpu.VMEM),
        scratch_shapes=[
            pltpu.VMEM((n, 8, 128), F32),
            pltpu.SemaphoreType.DMA((n,)),
            pltpu.SemaphoreType.DMA((n,)),
        ],
        compiler_params=pltpu.CompilerParams(collective_id=ident, has_side_effects=True),
    )(tile)
    return out[0, 0]


def day_major(matrix):
    n_days = matrix.shape[0]
    eye = jnp.eye(GROUP, dtype=BF)
    full = matrix[:, None, None, :] * eye[None, :, :, None]
    return full.reshape(GROUP * n_days, GROUP * n_days)


def lon_major(matrix):
    n_days = matrix.shape[0]
    eye = jnp.eye(GROUP, dtype=BF)
    full = matrix[None, :, :, None] * eye[:, None, None, :]
    return full.reshape(GROUP * n_days, GROUP * n_days)


def mm(spec, left, right):
    return jnp.einsum(spec, left, right, preferred_element_type=F32)


def to_exchanged(field, pieces):
    if pieces > 1:
        c, a, b = field.shape
        field = field.reshape(c, a, pieces, b // pieces).transpose(0, 2, 1, 3)
        field = field.reshape(c * pieces, a, b // pieces)
    return lax.all_to_all(field, "lon", split_axis=0, concat_axis=1, tiled=True)


def from_exchanged(wide, pieces):
    field = lax.all_to_all(wide, "lon", split_axis=1, concat_axis=0, tiled=True)
    if pieces > 1:
        cp, a, bp = field.shape
        field = field.reshape(cp // pieces, pieces, a, bp).transpose(0, 2, 1, 3)
        field = field.reshape(cp // pieces, a, bp * pieces)
    return field


def spread_products(field, day, lat_spec, lat):
    a, c, b = field.shape
    one = mm("rp,gpb->grb", day_major(day), field.reshape(a // GROUP, GROUP * c, b))
    two = mm(lat_spec, one.astype(BF), lat).astype(BF)
    two = two.reshape(a // GROUP, c, GROUP, b).transpose(1, 0, 2, 3)
    return two.reshape(c, a, b)


def on_device(
    n,
    solution,
    residual,
    direction,
    land,
    clear,
    days,
    mixture,
    q_lon,
    q_lat,
    q_day,
    lam_lon,
    lam_lat,
    lam_day,
    noise,
    rz_mean,
):
    shape = solution.shape
    lon_dev, n_days, n_lat = shape
    n_lon = q_lon.shape[0]
    cells = n_lon * n_days * n_lat
    pieces = max(1, n // n_days)
    observed = (land[:, None, :] * clear).astype(F32)
    sigma = noise[0]
    day_pos = days.astype(F32)
    k_lat = toeplitz_factor(n_lat, mixture[1])
    k_lon = toeplitz_factor(n_lon, mixture[0])
    k_day = kernel_values(day_pos[:, None] - day_pos[None, :], mixture[2]).astype(BF)

    first = (observed * direction).astype(BF)
    third = spread_products(first, k_day, "grj,bj->grb", k_lat)
    spread = to_exchanged(third, pieces)
    fourth = mm("ij,djb->dib", k_lon, spread).astype(BF)
    returned = from_exchanged(fourth, pieces).transpose(1, 0, 2)
    image = observed * (returned.astype(F32) + sigma * direction)
    curvature = all_sum(jnp.sum(direction * image), n, 1)
    alpha = rz_mean[0] * cells / curvature
    new_solution = solution + alpha * direction
    new_residual = residual - alpha * image

    g_zero = (observed * new_residual).astype(BF)
    g_two = spread_products(g_zero, q_day.T, "grj,jb->grb", q_lat)
    spread_g = to_exchanged(g_two, pieces)
    g_three = mm("ji,djb->dib", q_lon, spread_g).astype(BF)
    per = g_three.shape[0]
    width = n_lat // pieces
    at = lax.axis_index("lon")
    day_own = lax.dynamic_slice_in_dim(lam_day, at * per // pieces, per)
    lat_own = lax.dynamic_slice_in_dim(lam_lat, (at % pieces) * width, width)
    denom = lam_lon[None, :, None] * day_own[:, None, None] * lat_own[None, None, :] + sigma
    scaled = (g_three.astype(F32) / denom).astype(BF)
    h_one = mm("ij,djb->dib", q_lon, scaled).astype(BF)
    h_local = from_exchanged(h_one, pieces)
    h_two = mm("caj,bj->cab", h_local, q_lat).astype(BF)
    grouped = h_two.reshape(n_days, lon_dev // GROUP, GROUP, n_lat).transpose(1, 0, 2, 3)
    grouped = grouped.reshape(lon_dev // GROUP, n_days * GROUP, n_lat)
    last = mm("rp,gpb->grb", lon_major(q_day), grouped).reshape(shape)
    precond = observed * last
    total = all_sum(jnp.sum(new_residual * precond), n, 1)
    new_rz = total / cells
    new_direction = precond + new_rz / rz_mean[0] * direction
    return (new_solution, new_residual, new_direction, new_rz.reshape(1))


def solution(mesh):
    in_specs = (
        P(("parts", "lon"), None, None),
        P(("parts", "lon"), None, None),
        P(("parts", "lon"), None, None),
        P(("parts", "lon"), None),
        P(("parts", "lon"), None, None),
        P("parts"),
        P("parts", None, None),
        P(),
        P(),
        P("parts", None),
        P(),
        P(),
        P("parts"),
        P("parts"),
        P("parts"),
    )
    out_specs = (
        P(("parts", "lon"), None, None),
        P(("parts", "lon"), None, None),
        P(("parts", "lon"), None, None),
        P("parts"),
    )
    return jax.shard_map(
        functools.partial(on_device, mesh.shape["lon"]),
        mesh=mesh,
        in_specs=in_specs,
        out_specs=out_specs,
        check_vma=False,
    )
```

```python
import functools
import math

import jax
import jax.numpy as jnp
from jax import lax
from jax.experimental import pallas as pl
from jax.experimental.pallas import tpu as pltpu
from jax.sharding import PartitionSpec as P

GROUP = 16
BLOCK = 128
BF = jnp.bfloat16
F32 = jnp.float32


def factor_values(n_lon, n_lat, day_pos, mixture):
    lanes = 128
    lon_rows = 2 * n_lon // lanes
    lat_rows = 2 * n_lat // lanes
    n_days = day_pos.shape[0]
    lon_diff = (jnp.arange(2 * n_lon, dtype=F32) - n_lon).reshape(lon_rows, lanes)
    lat_diff = (jnp.arange(2 * n_lat, dtype=F32) - n_lat).reshape(lat_rows, lanes)
    day_diff = (day_pos[:, None] - day_pos[None, :]).reshape(-1, lanes)
    diff = jnp.concatenate([lon_diff, lat_diff, day_diff], axis=0)
    row = lax.broadcasted_iota(jnp.int32, diff.shape, 0)

    def pick(kind, comp):
        return jnp.where(
            row < lon_rows,
            mixture[0, kind, comp],
            jnp.where(
                row < lon_rows + lat_rows, mixture[1, kind, comp], mixture[2, kind, comp]
            ),
        )

    total = jnp.zeros(diff.shape, F32)
    for comp in range(mixture.shape[2]):
        ratio = diff / pick(2, comp)
        total = total + pick(0, comp) * jnp.exp(-0.5 * ratio * ratio) * jnp.cos(
            2.0 * math.pi * pick(1, comp) * diff
        )
    total = lax.optimization_barrier(total)
    lon = total[:lon_rows].reshape(1, 2 * n_lon)
    lat = total[lon_rows : lon_rows + lat_rows].reshape(1, 2 * n_lat)
    day = total[lon_rows + lat_rows :].reshape(n_days, n_days).astype(BF)
    return lon, lat, day


def toeplitz_kernel(w_ref, out_ref):
    n = out_ref.shape[0]
    wide = jnp.broadcast_to(w_ref[...], (BLOCK, 2 * n))
    rolled = pltpu.roll(wide, 0, 1, stride=1, stride_axis=0)
    for blk in range(n // BLOCK):
        lo = n - BLOCK * blk
        out_ref[BLOCK * blk : BLOCK * (blk + 1), :] = rolled[:, lo : lo + n].astype(BF)


def toeplitz_factor(row):
    n = row.shape[1] // 2
    return pl.pallas_call(
        toeplitz_kernel,
        out_shape=jax.ShapeDtypeStruct((n, n), BF),
        compiler_params=pltpu.CompilerParams(vmem_limit_bytes=24 * 1024 * 1024),
    )(row)


def allsum_kernel(n, x_ref, out_ref, buf, send_sem, recv_sem):
    me = lax.axis_index("lon")
    barrier = pltpu.get_barrier_semaphore()

    def greet(p, carry):
        peer = lax.rem(me + p, n)
        pl.semaphore_signal(
            barrier, inc=1, device_id={"lon": peer}, device_id_type=pl.DeviceIdType.MESH
        )
        return carry

    lax.fori_loop(1, n, greet, 0)
    pl.semaphore_wait(barrier, n - 1)

    def copy_to(p):
        return pltpu.make_async_remote_copy(
            src_ref=x_ref,
            dst_ref=buf.at[me],
            send_sem=send_sem.at[p],
            recv_sem=recv_sem.at[p],
            device_id={"lon": lax.rem(me + p, n)},
            device_id_type=pl.DeviceIdType.MESH,
        )

    def start(p, carry):
        copy_to(p).start()
        return carry

    lax.fori_loop(1, n, start, 0)
    buf[pl.ds(me, 1)] = x_ref[...][None]

    def finish(p, carry):
        copy_to(p).wait()
        return carry

    lax.fori_loop(1, n, finish, 0)
    out_ref[...] = jnp.sum(buf[...], axis=0)


def all_sum(value, n, ident):
    tile = jnp.full((8, 128), value, F32)
    out = pl.pallas_call(
        functools.partial(allsum_kernel, n),
        out_shape=jax.ShapeDtypeStruct((8, 128), F32),
        in_specs=[pl.BlockSpec(memory_space=pltpu.VMEM)],
        out_specs=pl.BlockSpec(memory_space=pltpu.VMEM),
        scratch_shapes=[
            pltpu.VMEM((n, 8, 128), F32),
            pltpu.SemaphoreType.DMA((n,)),
            pltpu.SemaphoreType.DMA((n,)),
        ],
        compiler_params=pltpu.CompilerParams(collective_id=ident, has_side_effects=True),
    )(tile)
    return out[0, 0]


def lon_kernel(n, scaled, *refs):
    if scaled:
        (x_ref, first_ref, second_ref, left_ref, lat_ref, sigma_ref, y_ref) = refs[:7]
        scratch = refs[7:]
    else:
        x_ref, first_ref, y_ref = refs[:3]
        scratch = refs[3:]
    got, res, mid, send_a, recv_a, send_b, recv_b = scratch
    per, n_lon, width = got.shape
    lon_dev = n_lon // n
    chunk = mid.shape[1]
    halves = width // chunk
    count = per * halves
    rows = min(256, n_lon)
    stride = max(1, n // 2 - 1)
    if math.gcd(stride, n) != 1:
        stride = 1
    me = lax.axis_index("lon")

    barrier = pltpu.get_barrier_semaphore()

    def greet(q, carry):
        pl.semaphore_signal(
            barrier,
            inc=1,
            device_id={"lon": lax.rem(me + q, n)},
            device_id_type=pl.DeviceIdType.MESH,
        )
        return carry

    lax.fori_loop(1, n, greet, 0)
    pl.semaphore_wait(barrier, n - 1)

    def place(k):
        return k // halves, pl.ds(pl.multiple_of((k % halves) * chunk, chunk), chunk)

    def lon_rows(dev):
        return pl.ds(pl.multiple_of(dev * lon_dev, lon_dev), lon_dev)

    def out_copy(k, q):
        r, cols = place(k)
        peer = lax.rem(me + q, n)
        return pltpu.make_async_remote_copy(
            src_ref=x_ref.at[peer * per + r, :, cols],
            dst_ref=got.at[r, lon_rows(me), cols],
            send_sem=send_a.at[k, q],
            recv_sem=recv_a.at[k, q],
            device_id={"lon": peer},
            device_id_type=pl.DeviceIdType.MESH,
        )

    def back_copy(k, q):
        r, cols = place(k)
        peer = lax.rem(me + q, n)
        return pltpu.make_async_remote_copy(
            src_ref=res.at[r, lon_rows(peer), cols],
            dst_ref=y_ref.at[me * per + r, :, cols],
            send_sem=send_b.at[k, q],
            recv_sem=recv_b.at[k, q],
            device_id={"lon": peer},
            device_id_type=pl.DeviceIdType.MESH,
        )

    def over_peers(body):
        def step(t, carry):
            body(lax.rem(t * stride, n))
            return carry

        lax.fori_loop(1, n, step, 0)

    def send_chunk(k, carry):
        over_peers(lambda q: out_copy(k, q).start())
        return carry

    lax.fori_loop(0, count, send_chunk, 0)

    def keep_own(k, carry):
        r, cols = place(k)
        got[r, lon_rows(me), cols] = x_ref[me * per + r, :, cols]
        return carry

    lax.fori_loop(0, count, keep_own, 0)

    def work(k, carry):
        r, cols = place(k)
        over_peers(lambda q: out_copy(k, q).wait_recv())

        def first(i, inner):
            at = pl.ds(pl.multiple_of(i * rows, rows), rows)
            prod = jnp.dot(first_ref[at, :], got[r, :, cols], preferred_element_type=F32)
            if scaled:
                g_three = prod.astype(BF).astype(F32)
                denom = left_ref[r, at, :] * lat_ref[:, cols] + sigma_ref[...]
                mid[at, :] = (g_three / denom).astype(BF)
            else:
                res[r, at, cols] = prod.astype(BF)
            return inner

        lax.fori_loop(0, n_lon // rows, first, 0)
        if scaled:

            def second(i, inner):
                at = pl.ds(pl.multiple_of(i * rows, rows), rows)
                res[r, at, cols] = jnp.dot(
                    second_ref[at, :], mid[...], preferred_element_type=F32
                ).astype(BF)
                return inner

            lax.fori_loop(0, n_lon // rows, second, 0)
        over_peers(lambda q: back_copy(k, q).start())
        y_ref[me * per + r, :, cols] = res[r, lon_rows(me), cols]
        return carry

    lax.fori_loop(0, count, work, 0)

    def finish(k, carry):
        over_peers(lambda q: out_copy(k, q).wait_send())
        over_peers(lambda q: back_copy(k, q).wait())
        return carry

    lax.fori_loop(0, count, finish, 0)


def lon_products(field, n, pieces, factors, scales, ident):
    c, a, b = field.shape
    n_lon = a * n
    if pieces > 1:
        field = field.reshape(c, a, pieces, b // pieces).transpose(0, 2, 1, 3)
        field = field.reshape(c * pieces, a, b // pieces)
    per = field.shape[0] // n
    width = field.shape[2]
    chunk = min(256, width)
    count = per * (width // chunk)
    vmem = pl.BlockSpec(memory_space=pltpu.VMEM)
    flops = 2 * len(factors) * n_lon * n_lon * per * width
    out = pl.pallas_call(
        functools.partial(lon_kernel, n, bool(scales)),
        out_shape=jax.ShapeDtypeStruct(field.shape, BF),
        in_specs=[vmem] * (1 + len(factors) + len(scales)),
        out_specs=vmem,
        scratch_shapes=[
            pltpu.VMEM((per, n_lon, width), BF),
            pltpu.VMEM((per, n_lon, width), BF),
            pltpu.VMEM((n_lon, chunk), BF),
            pltpu.SemaphoreType.DMA((count, n)),
            pltpu.SemaphoreType.DMA((count, n)),
            pltpu.SemaphoreType.DMA((count, n)),
            pltpu.SemaphoreType.DMA((count, n)),
        ],
        compiler_params=pltpu.CompilerParams(
            collective_id=ident, has_side_effects=True, vmem_limit_bytes=40 * 1024 * 1024
        ),
        cost_estimate=pl.CostEstimate(
            flops=flops, bytes_accessed=4 * field.size, transcendentals=0
        ),
    )(field, *factors, *scales)
    if pieces > 1:
        out = out.reshape(c, pieces, a, b // pieces).transpose(0, 2, 1, 3)
        out = out.reshape(c, a, b)
    return out


def day_major(matrix):
    n_days = matrix.shape[0]
    eye = jnp.eye(GROUP, dtype=BF)
    full = matrix[:, None, None, :] * eye[None, :, :, None]
    return full.reshape(GROUP * n_days, GROUP * n_days)


def lon_major(matrix):
    n_days = matrix.shape[0]
    eye = jnp.eye(GROUP, dtype=BF)
    full = matrix[None, :, :, None] * eye[:, None, None, :]
    return full.reshape(GROUP * n_days, GROUP * n_days)


def mm(spec, left, right):
    return jnp.einsum(spec, left, right, preferred_element_type=F32)


def spread_products(field, day, lat_spec, lat):
    a, c, b = field.shape
    one = mm("rp,gpb->grb", day_major(day), field.reshape(a // GROUP, GROUP * c, b))
    two = mm(lat_spec, one.astype(BF), lat).astype(BF)
    two = two.reshape(a // GROUP, c, GROUP, b).transpose(1, 0, 2, 3)
    return two.reshape(c, a, b)


def on_device(
    n,
    solution,
    residual,
    direction,
    land,
    clear,
    days,
    mixture,
    q_lon,
    q_lat,
    q_day,
    lam_lon,
    lam_lat,
    lam_day,
    noise,
    rz_mean,
):
    shape = solution.shape
    lon_dev, n_days, n_lat = shape
    n_lon = q_lon.shape[0]
    cells = n_lon * n_days * n_lat
    pieces = max(1, n // n_days)
    observed = (land[:, None, :] * clear).astype(F32)
    sigma = noise[0]
    day_pos = days.astype(F32)
    lon_row, lat_row, k_day = factor_values(n_lon, n_lat, day_pos, mixture)
    k_lat = toeplitz_factor(lat_row)
    k_lon = toeplitz_factor(lon_row)

    first = (observed * direction).astype(BF)
    third = spread_products(first, k_day, "grj,bj->grb", k_lat)
    fourth = lon_products(third, n, pieces, (k_lon,), (), 2)
    returned = fourth.transpose(1, 0, 2)
    image = observed * (returned.astype(F32) + sigma * direction)
    curvature = all_sum(jnp.sum(direction * image), n, 1)
    alpha = rz_mean[0] * cells / curvature
    new_solution = solution + alpha * direction
    new_residual = residual - alpha * image

    g_zero = (observed * new_residual).astype(BF)
    g_two = spread_products(g_zero, q_day.T, "grj,jb->grb", q_lat)
    per = n_days * pieces // n
    width = n_lat // pieces
    at = lax.axis_index("lon")
    day_own = lax.dynamic_slice_in_dim(lam_day, at * per // pieces, per)
    lat_own = lax.dynamic_slice_in_dim(lam_lat, (at % pieces) * width, width)
    left = lam_lon[None, :, None] * day_own[:, None, None]
    scales = (left, lat_own[None, :], sigma.reshape(1, 1))
    h_local = lon_products(g_two, n, pieces, (q_lon.T, q_lon), scales, 3)
    h_two = mm("caj,bj->cab", h_local, q_lat).astype(BF)
    grouped = h_two.reshape(n_days, lon_dev // GROUP, GROUP, n_lat).transpose(1, 0, 2, 3)
    grouped = grouped.reshape(lon_dev // GROUP, n_days * GROUP, n_lat)
    last = mm("rp,gpb->grb", lon_major(q_day), grouped).reshape(shape)
    precond = observed * last
    total = all_sum(jnp.sum(new_residual * precond), n, 1)
    new_rz = total / cells
    new_direction = precond + new_rz / rz_mean[0] * direction
    return (new_solution, new_residual, new_direction, new_rz.reshape(1))


def solution(mesh):
    in_specs = (
        P(("parts", "lon"), None, None),
        P(("parts", "lon"), None, None),
        P(("parts", "lon"), None, None),
        P(("parts", "lon"), None),
        P(("parts", "lon"), None, None),
        P("parts"),
        P("parts", None, None),
        P(),
        P(),
        P("parts", None),
        P(),
        P(),
        P("parts"),
        P("parts"),
        P("parts"),
    )
    out_specs = (
        P(("parts", "lon"), None, None),
        P(("parts", "lon"), None, None),
        P(("parts", "lon"), None, None),
        P("parts"),
    )
    return jax.shard_map(
        functools.partial(on_device, mesh.shape["lon"]),
        mesh=mesh,
        in_specs=in_specs,
        out_specs=out_specs,
        check_vma=False,
    )
```

```python
import functools
import math

import jax
import jax.numpy as jnp
from jax import lax
from jax.experimental import pallas as pl
from jax.experimental.pallas import tpu as pltpu
from jax.sharding import PartitionSpec as P

GROUP = 16
BLOCK = 128
BF = jnp.bfloat16
F32 = jnp.float32


def kernel_values(diff, mix_ref, dim, comps):
    total = jnp.zeros(diff.shape, F32)
    for comp in range(comps):
        weight = mix_ref[dim * 3 * comps + comp]
        freq = mix_ref[dim * 3 * comps + comps + comp]
        length = mix_ref[dim * 3 * comps + 2 * comps + comp]
        ratio = diff / length
        total = total + weight * jnp.exp(-0.5 * ratio * ratio) * jnp.cos(
            2.0 * math.pi * freq * diff
        )
    return total


def fill_toeplitz(out_ref, mix_ref, dim, comps):
    n = out_ref.shape[0]
    diff = (lax.broadcasted_iota(jnp.int32, (1, 2 * n), 1) - n).astype(F32)
    row = kernel_values(diff, mix_ref, dim, comps)
    rolled = pltpu.roll(
        jnp.broadcast_to(row, (BLOCK, 2 * n)), 0, 1, stride=1, stride_axis=0
    )
    for blk in range(n // BLOCK):
        lo = n - BLOCK * blk
        out_ref[BLOCK * blk : BLOCK * (blk + 1), :] = rolled[:, lo : lo + n].astype(BF)


def split(index, low):
    return lax.shift_right_logical(index, low.bit_length() - 1), index & (low - 1)


def block_diagonal(matrix, rows_day_first, cols_day_first):
    n_days = matrix.shape[0]
    size = n_days * GROUP

    def day_lon(index, day_first):
        if day_first:
            return split(index, GROUP)
        lon, day = split(index, n_days)
        return day, lon

    def iota(shape, dim):
        return lax.broadcasted_iota(jnp.int32, shape, dim)

    tall, flat, full = (size, n_days), (n_days, size), (size, size)
    pick_row = day_lon(iota(tall, 0), rows_day_first)[0] == iota(tall, 1)
    pick_col = day_lon(iota(flat, 1), cols_day_first)[0] == iota(flat, 0)
    pick_row = jnp.where(pick_row, 1.0, 0.0).astype(BF)
    pick_col = jnp.where(pick_col, 1.0, 0.0).astype(BF)
    spread = jnp.dot(pick_row, matrix, preferred_element_type=F32).astype(BF)
    spread = jnp.dot(spread, pick_col, preferred_element_type=F32)
    same = day_lon(iota(full, 0), rows_day_first)[1] == day_lon(iota(full, 1), cols_day_first)[1]
    return jnp.where(same, spread, 0.0).astype(BF)


def factor_kernel(
    comps, mix_ref, col_ref, row_ref, q_ref, qt_ref, lat_ref, lon_ref, k_ref, g_ref, h_ref, p_ref
):
    n_days = q_ref.shape[0]
    fill_toeplitz(lat_ref, mix_ref, 1, comps)
    fill_toeplitz(lon_ref, mix_ref, 0, comps)
    k_day = kernel_values(col_ref[...] - row_ref[...], mix_ref, 2, comps).astype(BF)
    k_ref[...] = block_diagonal(k_day, True, False)
    g_ref[...] = block_diagonal(qt_ref[...], True, False)
    h_ref[...] = block_diagonal(q_ref[...], False, True)
    shape = (n_days, n_days)
    eye = lax.broadcasted_iota(jnp.int32, shape, 0) == lax.broadcasted_iota(jnp.int32, shape, 1)
    p_ref[...] = block_diagonal(jnp.where(eye, 1.0, 0.0).astype(BF), False, True)


def factors(n_lon, n_lat, days, mixture, q_day):
    n_days = days.shape[0]
    size = GROUP * n_days
    pos = days.astype(F32)
    vmem = pl.BlockSpec(memory_space=pltpu.VMEM)
    square = jax.ShapeDtypeStruct((size, size), BF)
    return pl.pallas_call(
        functools.partial(factor_kernel, mixture.shape[2]),
        out_shape=[
            jax.ShapeDtypeStruct((n_lat, n_lat), BF),
            jax.ShapeDtypeStruct((n_lon, n_lon), BF),
            square,
            square,
            square,
            square,
        ],
        in_specs=[pl.BlockSpec(memory_space=pltpu.SMEM)] + [vmem] * 4,
        out_specs=[vmem] * 6,
        compiler_params=pltpu.CompilerParams(vmem_limit_bytes=40 * 1024 * 1024),
    )(mixture.reshape(-1), pos[:, None], pos[None, :], q_day, q_day.T)


def dot(left, right):
    return jnp.dot(left, right, preferred_element_type=F32)


def seen(land_ref, clear_ref):
    return (land_ref[...][:, None, :] * clear_ref[...]).astype(F32)


def fold(values):
    wide = jnp.sum(values.reshape(-1, 8, values.shape[-1]), axis=0)
    total = wide[:, 0:128]
    for at in range(128, wide.shape[1], 128):
        total = total + wide[:, at : at + 128]
    return total


def whole_sum(tile_ref):
    return jnp.sum(jnp.sum(tile_ref[...], axis=1, keepdims=True), axis=0, keepdims=True)


def add_tile(sum_ref, tile):
    @pl.when(pl.program_id(0) == 0)
    def _():
        sum_ref[...] = jnp.zeros_like(sum_ref)

    sum_ref[...] += tile


def front(field, day_ref, lat_ref, out_ref):
    a, c, b = field.shape
    one = dot(day_ref[...], field.astype(BF).reshape(a * c, b)).astype(BF)
    out_ref[...] = dot(one, lat_ref[...]).astype(BF).reshape(c, a, b)


def front_kernel(dir_ref, land_ref, clear_ref, day_ref, lat_ref, out_ref):
    front(seen(land_ref, clear_ref) * dir_ref[...], day_ref, lat_ref, out_ref)


def image_kernel(noise_ref, u_ref, dir_ref, land_ref, clear_ref, p_ref, image_ref, sum_ref):
    c, a, b = u_ref.shape
    back = dot(p_ref[...], u_ref[...].reshape(c * a, b)).reshape(a, c, b)
    direction = dir_ref[...]
    image = seen(land_ref, clear_ref) * (back + noise_ref[0] * direction)
    image_ref[...] = image
    add_tile(sum_ref, fold(direction * image))


def update_kernel(
    cells, rz_ref, sum_ref, image_ref, dir_ref, sol_ref, res_ref, land_ref, clear_ref,
    day_ref, lat_ref, new_sol_ref, new_res_ref, out_ref,
):
    alpha = rz_ref[0] * cells / whole_sum(sum_ref)
    alpha = alpha[:, :, None]
    new_sol_ref[...] = sol_ref[...] + alpha * dir_ref[...]
    new_res = res_ref[...] - alpha * image_ref[...]
    new_res_ref[...] = new_res
    front(seen(land_ref, clear_ref) * new_res, day_ref, lat_ref, out_ref)


def precond_kernel(h_ref, res_ref, land_ref, clear_ref, day_ref, lat_ref, out_ref, sum_ref):
    c, a, b = h_ref.shape
    two = lax.dot_general(
        h_ref[...].reshape(c * a, b),
        lat_ref[...],
        (((1,), (1,)), ((), ())),
        preferred_element_type=F32,
    ).astype(BF)
    precond = seen(land_ref, clear_ref) * dot(day_ref[...], two).reshape(a, c, b)
    out_ref[...] = precond
    add_tile(sum_ref, fold(res_ref[...] * precond))


def direction_kernel(cells, rz_ref, sum_ref, pre_ref, dir_ref, out_ref):
    ratio = (whole_sum(sum_ref) / cells) / rz_ref[0]
    out_ref[...] = pre_ref[...] + ratio[:, :, None] * dir_ref[...]


def blocked(kernel, steps, ins, outs):
    specs = {
        "s": lambda shape: pl.BlockSpec(memory_space=pltpu.SMEM),
        "w": lambda shape: pl.BlockSpec(shape, lambda i: (0, 0)),
        "f": lambda shape: pl.BlockSpec((GROUP,) + shape[1:], lambda i: (i, 0, 0)),
        "e": lambda shape: pl.BlockSpec((shape[0], GROUP, shape[2]), lambda i: (0, i, 0)),
        "m": lambda shape: pl.BlockSpec((GROUP, shape[1]), lambda i: (i, 0)),
    }
    return pl.pallas_call(
        kernel,
        grid=(steps,),
        in_specs=[specs[form](array.shape) for form, array in ins],
        out_specs=[specs[form](shape) for form, shape, _ in outs],
        out_shape=[jax.ShapeDtypeStruct(shape, kind) for _, shape, kind in outs],
        compiler_params=pltpu.CompilerParams(vmem_limit_bytes=48 * 1024 * 1024),
    )(*[array for _, array in ins])


def allsum_kernel(n, x_ref, out_ref, buf, send_sem, recv_sem):
    me = lax.axis_index("lon")
    barrier = pltpu.get_barrier_semaphore()

    def greet(p, carry):
        peer = lax.rem(me + p, n)
        pl.semaphore_signal(
            barrier, inc=1, device_id={"lon": peer}, device_id_type=pl.DeviceIdType.MESH
        )
        return carry

    lax.fori_loop(1, n, greet, 0)
    pl.semaphore_wait(barrier, n - 1)

    def copy_to(p):
        return pltpu.make_async_remote_copy(
            src_ref=x_ref,
            dst_ref=buf.at[me],
            send_sem=send_sem.at[p],
            recv_sem=recv_sem.at[p],
            device_id={"lon": lax.rem(me + p, n)},
            device_id_type=pl.DeviceIdType.MESH,
        )

    def start(p, carry):
        copy_to(p).start()
        return carry

    lax.fori_loop(1, n, start, 0)
    buf[pl.ds(me, 1)] = x_ref[...][None]

    def finish(p, carry):
        copy_to(p).wait()
        return carry

    lax.fori_loop(1, n, finish, 0)
    out_ref[...] = jnp.sum(buf[...], axis=0)


def all_sum(tile, n, ident):
    return pl.pallas_call(
        functools.partial(allsum_kernel, n),
        out_shape=jax.ShapeDtypeStruct((8, 128), F32),
        in_specs=[pl.BlockSpec(memory_space=pltpu.VMEM)],
        out_specs=pl.BlockSpec(memory_space=pltpu.VMEM),
        scratch_shapes=[
            pltpu.VMEM((n, 8, 128), F32),
            pltpu.SemaphoreType.DMA((n,)),
            pltpu.SemaphoreType.DMA((n,)),
        ],
        compiler_params=pltpu.CompilerParams(collective_id=ident, has_side_effects=True),
    )(tile)


def lon_kernel(n, scaled, *refs):
    if scaled:
        (x_ref, first_ref, second_ref, left_ref, lat_ref, sigma_ref, y_ref) = refs[:7]
        scratch = refs[7:]
    else:
        x_ref, first_ref, y_ref = refs[:3]
        scratch = refs[3:]
    got, res, mid, send_a, recv_a, send_b, recv_b = scratch
    per, n_lon, width = got.shape
    lon_dev = n_lon // n
    chunk = mid.shape[1]
    halves = width // chunk
    count = per * halves
    rows = min(256, n_lon)
    stride = max(1, n // 2 - 1)
    if math.gcd(stride, n) != 1:
        stride = 1
    me = lax.axis_index("lon")

    barrier = pltpu.get_barrier_semaphore()

    def greet(q, carry):
        pl.semaphore_signal(
            barrier,
            inc=1,
            device_id={"lon": lax.rem(me + q, n)},
            device_id_type=pl.DeviceIdType.MESH,
        )
        return carry

    lax.fori_loop(1, n, greet, 0)
    pl.semaphore_wait(barrier, n - 1)

    def place(k):
        return k // halves, pl.ds(pl.multiple_of((k % halves) * chunk, chunk), chunk)

    def lon_rows(dev):
        return pl.ds(pl.multiple_of(dev * lon_dev, lon_dev), lon_dev)

    def out_copy(k, q):
        r, cols = place(k)
        peer = lax.rem(me + q, n)
        return pltpu.make_async_remote_copy(
            src_ref=x_ref.at[peer * per + r, :, cols],
            dst_ref=got.at[r, lon_rows(me), cols],
            send_sem=send_a.at[k, q],
            recv_sem=recv_a.at[k, q],
            device_id={"lon": peer},
            device_id_type=pl.DeviceIdType.MESH,
        )

    def back_copy(k, q):
        r, cols = place(k)
        peer = lax.rem(me + q, n)
        return pltpu.make_async_remote_copy(
            src_ref=res.at[r, lon_rows(peer), cols],
            dst_ref=y_ref.at[me * per + r, :, cols],
            send_sem=send_b.at[k, q],
            recv_sem=recv_b.at[k, q],
            device_id={"lon": peer},
            device_id_type=pl.DeviceIdType.MESH,
        )

    def over_peers(body):
        def step(t, carry):
            body(lax.rem(t * stride, n))
            return carry

        lax.fori_loop(1, n, step, 0)

    def send_chunk(k, carry):
        over_peers(lambda q: out_copy(k, q).start())
        return carry

    lax.fori_loop(0, count, send_chunk, 0)

    def keep_own(k, carry):
        r, cols = place(k)
        got[r, lon_rows(me), cols] = x_ref[me * per + r, :, cols]
        return carry

    lax.fori_loop(0, count, keep_own, 0)

    def work(k, carry):
        r, cols = place(k)
        over_peers(lambda q: out_copy(k, q).wait_recv())

        def first(i, inner):
            at = pl.ds(pl.multiple_of(i * rows, rows), rows)
            prod = jnp.dot(first_ref[at, :], got[r, :, cols], preferred_element_type=F32)
            if scaled:
                g_three = prod.astype(BF).astype(F32)
                denom = left_ref[r, at, :] * lat_ref[:, cols] + sigma_ref[...]
                mid[at, :] = (g_three / denom).astype(BF)
            else:
                res[r, at, cols] = prod.astype(BF)
            return inner

        lax.fori_loop(0, n_lon // rows, first, 0)
        if scaled:

            def second(i, inner):
                at = pl.ds(pl.multiple_of(i * rows, rows), rows)
                res[r, at, cols] = jnp.dot(
                    second_ref[at, :], mid[...], preferred_element_type=F32
                ).astype(BF)
                return inner

            lax.fori_loop(0, n_lon // rows, second, 0)
        over_peers(lambda q: back_copy(k, q).start())
        y_ref[me * per + r, :, cols] = res[r, lon_rows(me), cols]
        return carry

    lax.fori_loop(0, count, work, 0)

    def finish(k, carry):
        over_peers(lambda q: out_copy(k, q).wait_send())
        over_peers(lambda q: back_copy(k, q).wait())
        return carry

    lax.fori_loop(0, count, finish, 0)


def lon_products(field, n, pieces, factors, scales, ident):
    c, a, b = field.shape
    n_lon = a * n
    if pieces > 1:
        field = field.reshape(c, a, pieces, b // pieces).transpose(0, 2, 1, 3)
        field = field.reshape(c * pieces, a, b // pieces)
    per = field.shape[0] // n
    width = field.shape[2]
    chunk = min(256, width)
    count = per * (width // chunk)
    vmem = pl.BlockSpec(memory_space=pltpu.VMEM)
    flops = 2 * len(factors) * n_lon * n_lon * per * width
    out = pl.pallas_call(
        functools.partial(lon_kernel, n, bool(scales)),
        out_shape=jax.ShapeDtypeStruct(field.shape, BF),
        in_specs=[vmem] * (1 + len(factors) + len(scales)),
        out_specs=vmem,
        scratch_shapes=[
            pltpu.VMEM((per, n_lon, width), BF),
            pltpu.VMEM((per, n_lon, width), BF),
            pltpu.VMEM((n_lon, chunk), BF),
            pltpu.SemaphoreType.DMA((count, n)),
            pltpu.SemaphoreType.DMA((count, n)),
            pltpu.SemaphoreType.DMA((count, n)),
            pltpu.SemaphoreType.DMA((count, n)),
        ],
        compiler_params=pltpu.CompilerParams(
            collective_id=ident, has_side_effects=True, vmem_limit_bytes=40 * 1024 * 1024
        ),
        cost_estimate=pl.CostEstimate(
            flops=flops, bytes_accessed=4 * field.size, transcendentals=0
        ),
    )(field, *factors, *scales)
    if pieces > 1:
        out = out.reshape(c, pieces, a, b // pieces).transpose(0, 2, 1, 3)
        out = out.reshape(c, a, b)
    return out


def day_major(matrix):
    n_days = matrix.shape[0]
    eye = jnp.eye(GROUP, dtype=BF)
    full = matrix[:, None, None, :] * eye[None, :, :, None]
    return full.reshape(GROUP * n_days, GROUP * n_days)


def lon_major(matrix):
    n_days = matrix.shape[0]
    eye = jnp.eye(GROUP, dtype=BF)
    full = matrix[None, :, :, None] * eye[:, None, None, :]
    return full.reshape(GROUP * n_days, GROUP * n_days)


def mm(spec, left, right):
    return jnp.einsum(spec, left, right, preferred_element_type=F32)


def on_device(
    n,
    solution,
    residual,
    direction,
    land,
    clear,
    days,
    mixture,
    q_lon,
    q_lat,
    q_day,
    lam_lon,
    lam_lat,
    lam_day,
    noise,
    rz_mean,
):
    shape = solution.shape
    lon_dev, n_days, n_lat = shape
    n_lon = q_lon.shape[0]
    cells = n_lon * n_days * n_lat
    pieces = max(1, n // n_days)
    steps = lon_dev // GROUP
    by_day = (n_days, lon_dev, n_lat)
    tile = ("w", (8, 128), F32)
    k_lat, k_lon, k_mix, g_mix, h_mix, permute = factors(n_lon, n_lat, days, mixture, q_day)

    masks = [("m", land), ("f", clear)]
    (third,) = blocked(
        front_kernel,
        steps,
        [("f", direction), *masks, ("w", k_mix), ("w", k_lat)],
        [("e", by_day, BF)],
    )
    fourth = lon_products(third, n, pieces, (k_lon,), (), 2)
    image, partial = blocked(
        image_kernel,
        steps,
        [("s", noise), ("e", fourth), ("f", direction), *masks, ("w", permute)],
        [("f", shape, F32), tile],
    )
    curvature = all_sum(partial, n, 1)
    new_solution, new_residual, g_two = blocked(
        functools.partial(update_kernel, float(cells)),
        steps,
        [
            ("s", rz_mean),
            ("w", curvature),
            ("f", image),
            ("f", direction),
            ("f", solution),
            ("f", residual),
            *masks,
            ("w", g_mix),
            ("w", q_lat),
        ],
        [("f", shape, F32), ("f", shape, F32), ("e", by_day, BF)],
    )

    per = n_days * pieces // n
    width = n_lat // pieces
    at = lax.axis_index("lon")
    day_own = lax.dynamic_slice_in_dim(lam_day, at * per // pieces, per)
    lat_own = lax.dynamic_slice_in_dim(lam_lat, (at % pieces) * width, width)
    left = lam_lon[None, :, None] * day_own[:, None, None]
    scales = (left, lat_own[None, :], noise.reshape(1, 1))
    h_local = lon_products(g_two, n, pieces, (q_lon.T, q_lon), scales, 3)
    precond, partial = blocked(
        precond_kernel,
        steps,
        [("e", h_local), ("f", new_residual), *masks, ("w", h_mix), ("w", q_lat)],
        [("f", shape, F32), tile],
    )
    total = all_sum(partial, n, 1)
    (new_direction,) = blocked(
        functools.partial(direction_kernel, float(cells)),
        steps,
        [("s", rz_mean), ("w", total), ("f", precond), ("f", direction)],
        [("f", shape, F32)],
    )
    new_rz = jnp.sum(total) / cells
    return (new_solution, new_residual, new_direction, new_rz.reshape(1))


def solution(mesh):
    in_specs = (
        P(("parts", "lon"), None, None),
        P(("parts", "lon"), None, None),
        P(("parts", "lon"), None, None),
        P(("parts", "lon"), None),
        P(("parts", "lon"), None, None),
        P("parts"),
        P("parts", None, None),
        P(),
        P(),
        P("parts", None),
        P(),
        P(),
        P("parts"),
        P("parts"),
        P("parts"),
    )
    out_specs = (
        P(("parts", "lon"), None, None),
        P(("parts", "lon"), None, None),
        P(("parts", "lon"), None, None),
        P("parts"),
    )
    return jax.shard_map(
        functools.partial(on_device, mesh.shape["lon"]),
        mesh=mesh,
        in_specs=in_specs,
        out_specs=out_specs,
        check_vma=False,
    )
```

```python
import functools
import math

import jax
import jax.numpy as jnp
from jax import lax
from jax.experimental import pallas as pl
from jax.experimental.pallas import tpu as pltpu
from jax.sharding import PartitionSpec as P

GROUP = 16
BLOCK = 128
BF = jnp.bfloat16
F32 = jnp.float32


def kernel_values(diff, mix_ref, dim, comps):
    total = jnp.zeros(diff.shape, F32)
    for comp in range(comps):
        weight = mix_ref[dim * 3 * comps + comp]
        freq = mix_ref[dim * 3 * comps + comps + comp]
        length = mix_ref[dim * 3 * comps + 2 * comps + comp]
        ratio = diff / length
        total = total + weight * jnp.exp(-0.5 * ratio * ratio) * jnp.cos(
            2.0 * math.pi * freq * diff
        )
    return total


def fill_toeplitz(out_ref, mix_ref, dim, comps):
    n = out_ref.shape[0]
    diff = (lax.broadcasted_iota(jnp.int32, (1, 2 * n), 1) - n).astype(F32)
    row = kernel_values(diff, mix_ref, dim, comps)
    rolled = pltpu.roll(
        jnp.broadcast_to(row, (BLOCK, 2 * n)), 0, 1, stride=1, stride_axis=0
    )
    for blk in range(n // BLOCK):
        lo = n - BLOCK * blk
        out_ref[BLOCK * blk : BLOCK * (blk + 1), :] = rolled[:, lo : lo + n].astype(BF)


def split(index, low):
    return lax.shift_right_logical(index, low.bit_length() - 1), index & (low - 1)


def block_diagonal(matrix, rows_day_first, cols_day_first):
    n_days = matrix.shape[0]
    size = n_days * GROUP

    def day_lon(index, day_first):
        if day_first:
            return split(index, GROUP)
        lon, day = split(index, n_days)
        return day, lon

    def iota(shape, dim):
        return lax.broadcasted_iota(jnp.int32, shape, dim)

    tall, flat, full = (size, n_days), (n_days, size), (size, size)
    pick_row = day_lon(iota(tall, 0), rows_day_first)[0] == iota(tall, 1)
    pick_col = day_lon(iota(flat, 1), cols_day_first)[0] == iota(flat, 0)
    pick_row = jnp.where(pick_row, 1.0, 0.0).astype(BF)
    pick_col = jnp.where(pick_col, 1.0, 0.0).astype(BF)
    spread = jnp.dot(pick_row, matrix, preferred_element_type=F32).astype(BF)
    spread = jnp.dot(spread, pick_col, preferred_element_type=F32)
    same = day_lon(iota(full, 0), rows_day_first)[1] == day_lon(iota(full, 1), cols_day_first)[1]
    return jnp.where(same, spread, 0.0).astype(BF)


def factor_kernel(
    comps, mix_ref, col_ref, row_ref, q_ref, qt_ref, lat_ref, lon_ref, k_ref, g_ref, h_ref, p_ref
):
    n_days = q_ref.shape[0]
    fill_toeplitz(lat_ref, mix_ref, 1, comps)
    fill_toeplitz(lon_ref, mix_ref, 0, comps)
    k_day = kernel_values(col_ref[...] - row_ref[...], mix_ref, 2, comps).astype(BF)
    k_ref[...] = block_diagonal(k_day, True, False)
    g_ref[...] = block_diagonal(qt_ref[...], True, False)
    h_ref[...] = block_diagonal(q_ref[...], False, True)
    shape = (n_days, n_days)
    eye = lax.broadcasted_iota(jnp.int32, shape, 0) == lax.broadcasted_iota(jnp.int32, shape, 1)
    p_ref[...] = block_diagonal(jnp.where(eye, 1.0, 0.0).astype(BF), False, True)


def factors(n_lon, n_lat, days, mixture, q_day):
    n_days = days.shape[0]
    size = GROUP * n_days
    pos = days.astype(F32)
    vmem = pl.BlockSpec(memory_space=pltpu.VMEM)
    square = jax.ShapeDtypeStruct((size, size), BF)
    return pl.pallas_call(
        functools.partial(factor_kernel, mixture.shape[2]),
        out_shape=[
            jax.ShapeDtypeStruct((n_lat, n_lat), BF),
            jax.ShapeDtypeStruct((n_lon, n_lon), BF),
            square,
            square,
            square,
            square,
        ],
        in_specs=[pl.BlockSpec(memory_space=pltpu.SMEM)] + [vmem] * 4,
        out_specs=[vmem] * 6,
        compiler_params=pltpu.CompilerParams(vmem_limit_bytes=40 * 1024 * 1024),
    )(mixture.reshape(-1), pos[:, None], pos[None, :], q_day, q_day.T)


def dot(left, right):
    return jnp.dot(left, right, preferred_element_type=F32)


def seen(land_ref, clear_ref):
    return (land_ref[...][:, None, :] * clear_ref[...]).astype(F32)


def fold(values):
    wide = jnp.sum(values.reshape(-1, 8, values.shape[-1]), axis=0)
    total = wide[:, 0:128]
    for at in range(128, wide.shape[1], 128):
        total = total + wide[:, at : at + 128]
    return total


def whole_sum(tile_ref):
    return jnp.sum(jnp.sum(tile_ref[...], axis=1, keepdims=True), axis=0, keepdims=True)


def greet_peers(n):
    me = lax.axis_index("lon")
    barrier = pltpu.get_barrier_semaphore()

    def greet(q, carry):
        pl.semaphore_signal(
            barrier,
            inc=1,
            device_id={"lon": lax.rem(me + q, n)},
            device_id_type=pl.DeviceIdType.MESH,
        )
        return carry

    lax.fori_loop(1, n, greet, 0)


def greet_first(n):
    @pl.when(pl.program_id(0) == 0)
    def _():
        greet_peers(n)


def sum_tiles(n, tile, sum_ref, own, buf, send_sem, recv_sem):
    step = pl.program_id(0)

    @pl.when(step == 0)
    def _():
        own[...] = jnp.zeros_like(own)

    own[...] += tile

    @pl.when(step == pl.num_programs(0) - 1)
    def _():
        me = lax.axis_index("lon")
        pl.semaphore_wait(pltpu.get_barrier_semaphore(), n - 1)

        def copy_to(q):
            return pltpu.make_async_remote_copy(
                src_ref=own,
                dst_ref=buf.at[me],
                send_sem=send_sem.at[q],
                recv_sem=recv_sem.at[q],
                device_id={"lon": lax.rem(me + q, n)},
                device_id_type=pl.DeviceIdType.MESH,
            )

        def start(q, carry):
            copy_to(q).start()
            return carry

        def finish(q, carry):
            copy_to(q).wait()
            return carry

        lax.fori_loop(1, n, start, 0)
        buf[pl.ds(me, 1)] = own[...][None]
        lax.fori_loop(1, n, finish, 0)
        sum_ref[...] = jnp.sum(buf[...], axis=0)


def front(field, day_ref, lat_ref, out_ref):
    a, c, b = field.shape
    one = dot(day_ref[...], field.astype(BF).reshape(a * c, b)).astype(BF)
    out_ref[...] = dot(one, lat_ref[...]).astype(BF).reshape(c, a, b)


def front_kernel(dir_ref, land_ref, clear_ref, day_ref, lat_ref, out_ref):
    front(seen(land_ref, clear_ref) * dir_ref[...], day_ref, lat_ref, out_ref)


def image_kernel(
    n, noise_ref, u_ref, dir_ref, land_ref, clear_ref, p_ref, image_ref, sum_ref, *scratch
):
    greet_first(n)
    c, a, b = u_ref.shape
    back = dot(p_ref[...], u_ref[...].reshape(c * a, b)).reshape(a, c, b)
    direction = dir_ref[...]
    image = seen(land_ref, clear_ref) * (back + noise_ref[0] * direction)
    image_ref[...] = image
    sum_tiles(n, fold(direction * image), sum_ref, *scratch)


def update_kernel(
    cells, rz_ref, sum_ref, image_ref, dir_ref, sol_ref, res_ref, land_ref, clear_ref,
    day_ref, lat_ref, new_sol_ref, new_res_ref, out_ref,
):
    alpha = rz_ref[0] * cells / whole_sum(sum_ref)
    alpha = alpha[:, :, None]
    new_sol_ref[...] = sol_ref[...] + alpha * dir_ref[...]
    new_res = res_ref[...] - alpha * image_ref[...]
    new_res_ref[...] = new_res
    front(seen(land_ref, clear_ref) * new_res, day_ref, lat_ref, out_ref)


def precond_kernel(
    n, h_ref, res_ref, land_ref, clear_ref, day_ref, lat_ref, out_ref, sum_ref, *scratch
):
    greet_first(n)
    c, a, b = h_ref.shape
    two = lax.dot_general(
        h_ref[...].reshape(c * a, b),
        lat_ref[...],
        (((1,), (1,)), ((), ())),
        preferred_element_type=F32,
    ).astype(BF)
    precond = seen(land_ref, clear_ref) * dot(day_ref[...], two).reshape(a, c, b)
    out_ref[...] = precond
    sum_tiles(n, fold(res_ref[...] * precond), sum_ref, *scratch)


def direction_kernel(cells, rz_ref, sum_ref, pre_ref, dir_ref, out_ref):
    ratio = (whole_sum(sum_ref) / cells) / rz_ref[0]
    out_ref[...] = pre_ref[...] + ratio[:, :, None] * dir_ref[...]


def blocked(kernel, steps, ins, outs, n=0, ident=None):
    specs = {
        "s": lambda shape: pl.BlockSpec(memory_space=pltpu.SMEM),
        "w": lambda shape: pl.BlockSpec(shape, lambda i: (0, 0)),
        "f": lambda shape: pl.BlockSpec((GROUP,) + shape[1:], lambda i: (i, 0, 0)),
        "e": lambda shape: pl.BlockSpec((shape[0], GROUP, shape[2]), lambda i: (0, i, 0)),
        "m": lambda shape: pl.BlockSpec((GROUP, shape[1]), lambda i: (i, 0)),
    }
    scratch, remote = [], {}
    if ident is not None:
        scratch = [
            pltpu.VMEM((8, 128), F32),
            pltpu.VMEM((n, 8, 128), F32),
            pltpu.SemaphoreType.DMA((n,)),
            pltpu.SemaphoreType.DMA((n,)),
        ]
        remote = dict(collective_id=ident, has_side_effects=True)
    return pl.pallas_call(
        kernel,
        grid=(steps,),
        scratch_shapes=scratch,
        in_specs=[specs[form](array.shape) for form, array in ins],
        out_specs=[specs[form](shape) for form, shape, _ in outs],
        out_shape=[jax.ShapeDtypeStruct(shape, kind) for _, shape, kind in outs],
        compiler_params=pltpu.CompilerParams(vmem_limit_bytes=48 * 1024 * 1024, **remote),
    )(*[array for _, array in ins])


def lon_kernel(n, scaled, *refs):
    if scaled:
        x_ref, second_ref, left_ref, lat_ref, sigma_ref, y_ref = refs[:6]
        first_ref = refs[-1]
        scratch = refs[6:-1]
    else:
        x_ref, first_ref, y_ref = refs[:3]
        scratch = refs[3:]
    got, res, mid, send_a, recv_a, send_b, recv_b = scratch
    per, n_lon, width = got.shape
    lon_dev = n_lon // n
    chunk = mid.shape[1]
    halves = width // chunk
    count = per * halves
    rows = min(256, n_lon)
    stride = max(1, n // 2 - 1)
    if math.gcd(stride, n) != 1:
        stride = 1
    me = lax.axis_index("lon")

    greet_peers(n)
    pl.semaphore_wait(pltpu.get_barrier_semaphore(), n - 1)

    def place(k):
        return k // halves, pl.ds(pl.multiple_of((k % halves) * chunk, chunk), chunk)

    def lon_rows(dev):
        return pl.ds(pl.multiple_of(dev * lon_dev, lon_dev), lon_dev)

    def out_copy(k, q):
        r, cols = place(k)
        peer = lax.rem(me + q, n)
        return pltpu.make_async_remote_copy(
            src_ref=x_ref.at[peer * per + r, :, cols],
            dst_ref=got.at[r, lon_rows(me), cols],
            send_sem=send_a.at[k, q],
            recv_sem=recv_a.at[k, q],
            device_id={"lon": peer},
            device_id_type=pl.DeviceIdType.MESH,
        )

    def back_copy(k, q):
        r, cols = place(k)
        peer = lax.rem(me + q, n)
        return pltpu.make_async_remote_copy(
            src_ref=res.at[r, lon_rows(peer), cols],
            dst_ref=y_ref.at[me * per + r, :, cols],
            send_sem=send_b.at[k, q],
            recv_sem=recv_b.at[k, q],
            device_id={"lon": peer},
            device_id_type=pl.DeviceIdType.MESH,
        )

    def over_peers(body):
        def step(t, carry):
            body(lax.rem(t * stride, n))
            return carry

        lax.fori_loop(1, n, step, 0)

    def send_chunk(k, carry):
        over_peers(lambda q: out_copy(k, q).start())
        return carry

    lax.fori_loop(0, count, send_chunk, 0)

    def keep_own(k, carry):
        r, cols = place(k)
        got[r, lon_rows(me), cols] = x_ref[me * per + r, :, cols]
        return carry

    lax.fori_loop(0, count, keep_own, 0)
    if scaled:

        def turn(i, carry):
            at = pl.ds(pl.multiple_of(i * rows, rows), rows)
            first_ref[at, :] = second_ref[:, at].T
            return carry

        lax.fori_loop(0, n_lon // rows, turn, 0)

    def work(k, carry):
        r, cols = place(k)
        over_peers(lambda q: out_copy(k, q).wait_recv())

        def first(i, inner):
            at = pl.ds(pl.multiple_of(i * rows, rows), rows)
            prod = jnp.dot(first_ref[at, :], got[r, :, cols], preferred_element_type=F32)
            if scaled:
                g_three = prod.astype(BF).astype(F32)
                denom = left_ref[r, at, :] * lat_ref[:, cols] + sigma_ref[...]
                mid[at, :] = (g_three / denom).astype(BF)
            else:
                res[r, at, cols] = prod.astype(BF)
            return inner

        lax.fori_loop(0, n_lon // rows, first, 0)
        if scaled:

            def second(i, inner):
                at = pl.ds(pl.multiple_of(i * rows, rows), rows)
                res[r, at, cols] = jnp.dot(
                    second_ref[at, :], mid[...], preferred_element_type=F32
                ).astype(BF)
                return inner

            lax.fori_loop(0, n_lon // rows, second, 0)
        over_peers(lambda q: back_copy(k, q).start())
        y_ref[me * per + r, :, cols] = res[r, lon_rows(me), cols]
        return carry

    lax.fori_loop(0, count, work, 0)

    def finish(k, carry):
        over_peers(lambda q: out_copy(k, q).wait_send())
        over_peers(lambda q: back_copy(k, q).wait())
        return carry

    lax.fori_loop(0, count, finish, 0)


def lon_products(field, n, pieces, factor, scales, ident):
    c, a, b = field.shape
    n_lon = a * n
    if pieces > 1:
        field = field.reshape(c, a, pieces, b // pieces).transpose(0, 2, 1, 3)
        field = field.reshape(c * pieces, a, b // pieces)
    per = field.shape[0] // n
    width = field.shape[2]
    chunk = min(256, width)
    count = per * (width // chunk)
    vmem = pl.BlockSpec(memory_space=pltpu.VMEM)
    flops = 2 * (2 if scales else 1) * n_lon * n_lon * per * width
    out = pl.pallas_call(
        functools.partial(lon_kernel, n, bool(scales)),
        out_shape=jax.ShapeDtypeStruct(field.shape, BF),
        in_specs=[vmem] * (2 + len(scales)),
        out_specs=vmem,
        scratch_shapes=[
            pltpu.VMEM((per, n_lon, width), BF),
            pltpu.VMEM((per, n_lon, width), BF),
            pltpu.VMEM((n_lon, chunk), BF),
            pltpu.SemaphoreType.DMA((count, n)),
            pltpu.SemaphoreType.DMA((count, n)),
            pltpu.SemaphoreType.DMA((count, n)),
            pltpu.SemaphoreType.DMA((count, n)),
        ]
        + ([pltpu.VMEM((n_lon, n_lon), BF)] if scales else []),
        compiler_params=pltpu.CompilerParams(
            collective_id=ident, has_side_effects=True, vmem_limit_bytes=40 * 1024 * 1024
        ),
        cost_estimate=pl.CostEstimate(
            flops=flops, bytes_accessed=4 * field.size, transcendentals=0
        ),
    )(field, factor, *scales)
    if pieces > 1:
        out = out.reshape(c, pieces, a, b // pieces).transpose(0, 2, 1, 3)
        out = out.reshape(c, a, b)
    return out


def day_major(matrix):
    n_days = matrix.shape[0]
    eye = jnp.eye(GROUP, dtype=BF)
    full = matrix[:, None, None, :] * eye[None, :, :, None]
    return full.reshape(GROUP * n_days, GROUP * n_days)


def lon_major(matrix):
    n_days = matrix.shape[0]
    eye = jnp.eye(GROUP, dtype=BF)
    full = matrix[None, :, :, None] * eye[:, None, None, :]
    return full.reshape(GROUP * n_days, GROUP * n_days)


def mm(spec, left, right):
    return jnp.einsum(spec, left, right, preferred_element_type=F32)


def on_device(
    n,
    solution,
    residual,
    direction,
    land,
    clear,
    days,
    mixture,
    q_lon,
    q_lat,
    q_day,
    lam_lon,
    lam_lat,
    lam_day,
    noise,
    rz_mean,
):
    shape = solution.shape
    lon_dev, n_days, n_lat = shape
    n_lon = q_lon.shape[0]
    cells = n_lon * n_days * n_lat
    pieces = max(1, n // n_days)
    steps = lon_dev // GROUP
    by_day = (n_days, lon_dev, n_lat)
    tile = ("w", (8, 128), F32)
    k_lat, k_lon, k_mix, g_mix, h_mix, permute = factors(n_lon, n_lat, days, mixture, q_day)

    masks = [("m", land), ("f", clear)]
    (third,) = blocked(
        front_kernel,
        steps,
        [("f", direction), *masks, ("w", k_mix), ("w", k_lat)],
        [("e", by_day, BF)],
    )
    fourth = lon_products(third, n, pieces, k_lon, (), 2)
    image, curvature = blocked(
        functools.partial(image_kernel, n),
        steps,
        [("s", noise), ("e", fourth), ("f", direction), *masks, ("w", permute)],
        [("f", shape, F32), tile],
        n,
        1,
    )
    new_solution, new_residual, g_two = blocked(
        functools.partial(update_kernel, float(cells)),
        steps,
        [
            ("s", rz_mean),
            ("w", curvature),
            ("f", image),
            ("f", direction),
            ("f", solution),
            ("f", residual),
            *masks,
            ("w", g_mix),
            ("w", q_lat),
        ],
        [("f", shape, F32), ("f", shape, F32), ("e", by_day, BF)],
    )

    per = n_days * pieces // n
    width = n_lat // pieces
    at = lax.axis_index("lon")
    day_own = lax.dynamic_slice_in_dim(lam_day, at * per // pieces, per)
    lat_own = lax.dynamic_slice_in_dim(lam_lat, (at % pieces) * width, width)
    left = lam_lon[None, :, None] * day_own[:, None, None]
    scales = (left, lat_own[None, :], noise.reshape(1, 1))
    h_local = lon_products(g_two, n, pieces, q_lon, scales, 3)
    precond, total = blocked(
        functools.partial(precond_kernel, n),
        steps,
        [("e", h_local), ("f", new_residual), *masks, ("w", h_mix), ("w", q_lat)],
        [("f", shape, F32), tile],
        n,
        4,
    )
    (new_direction,) = blocked(
        functools.partial(direction_kernel, float(cells)),
        steps,
        [("s", rz_mean), ("w", total), ("f", precond), ("f", direction)],
        [("f", shape, F32)],
    )
    new_rz = jnp.sum(total) / cells
    return (new_solution, new_residual, new_direction, new_rz.reshape(1))


def solution(mesh):
    in_specs = (
        P(("parts", "lon"), None, None),
        P(("parts", "lon"), None, None),
        P(("parts", "lon"), None, None),
        P(("parts", "lon"), None),
        P(("parts", "lon"), None, None),
        P("parts"),
        P("parts", None, None),
        P(),
        P(),
        P("parts", None),
        P(),
        P(),
        P("parts"),
        P("parts"),
        P("parts"),
    )
    out_specs = (
        P(("parts", "lon"), None, None),
        P(("parts", "lon"), None, None),
        P(("parts", "lon"), None, None),
        P("parts"),
    )
    return jax.shard_map(
        functools.partial(on_device, mesh.shape["lon"]),
        mesh=mesh,
        in_specs=in_specs,
        out_specs=out_specs,
        check_vma=False,
    )
```
